32 devices in a mesh: groups: 2 (over x), mx: 16 (over z, y, core).
Axes of the slice: x: 2, y: 2, z: 4, core: 2. Of those that a mesh axis runs over, the one named last changes fastest.
Arguments:
- tokens: bfloat16 [128, 18432], P('groups', 'mx'), parts along dimension 0
- norm_gain: bfloat16 [18432], P('mx'), may hold values from 0.099609375 to 1.8984375
- w_qkv: bfloat16 [18432, 8192], P(None, 'mx'), may hold values from -0.046875 to 0.046875
- key_cache: bfloat16 [128, 1024, 256], P(('groups', 'mx')), parts along dimension 0
- value_cache: bfloat16 [128, 1024, 256], P(('groups', 'mx')), parts along dimension 0, may hold values from -6 to 6
- lengths: int32 [128], P(('groups', 'mx')), parts along dimension 0, may hold values from 1 to 1024, as said below
- positions: int32 [128], P(('groups', 'mx')), parts along dimension 0, may hold values from 0 to 1023
- w_out: bfloat16 [7680, 18432], P(None, 'mx'), may hold values from -0.0625 to 0.0625
Outputs:
- mixed: bfloat16 [128, 18432], P('groups', 'mx'), parts along dimension 0
The draws below stay inside these ranges and needn't reach their ends.
There are 2 independent parts, one for each index of `groups`. The reference program is written for one: setup_inputs(seed, part) draws one part's arguments, and reference() takes and returns one part's arrays. A program takes and returns all parts, laid end to end along the dimension named above; an argument that names none is the same for every part. Nothing has to cross between parts.
Inputs may be any that keep to these rules, and one draw needn't show every extreme that they name: Each row attends to its first lengths cache slots; in every draw some row has exactly 1024.
All inputs are finite; a program needn't handle non-finite values.
Results may differ from the reference program's by a relative error of at most 0.0075.
The reference program's roundings to bfloat16 on the way (of `normed`, `joined` and `attended`) count: a program that leaves them out, or rounds other values in their place, can miss the bound.
Values may be sent and summed in bfloat16 or wider, within the bound.
A program may use at most 128 MiB of HBM per device.

```python
import math
import jax
import jax.numpy as jnp
from jax import lax

D = 18432
HQ = 30
DH = 256
CTX = 1024
ROWS = 64


def draw_tokens(key, part):
    key = jax.random.fold_in(key, 11)
    first_key, second_key, third_key, fourth_key = jax.random.split(key, 4)
    column_scale = jnp.power(3.0, 0.5 * jnp.arange(D, dtype=jnp.float32) / (D - 1))
    column_scale = column_scale * jax.random.uniform(second_key, (D,), jnp.float32, 0.7, 1.3)
    row_scale = jnp.exp(jax.random.uniform(third_key, (ROWS, 1), jnp.float32, 0.0, math.log(10.0)))
    offset = jax.random.uniform(fourth_key, (ROWS, 1), jnp.float32, -1.0, 1.0)
    base = jax.random.normal(first_key, (ROWS, D), jnp.float32)
    return ((base + offset) * column_scale[None, :] * row_scale).astype(jnp.bfloat16)


def draw_key_cache(key, part):
    key = jax.random.fold_in(key, 23)
    first_key = jax.random.fold_in(key, 0)
    values_out = jnp.clip(jax.random.normal(first_key, (ROWS, CTX, DH), jnp.float32), -6.0, 6.0)
    return values_out.astype(jnp.bfloat16)


def draw_lengths(key, part):
    key = jax.random.fold_in(key, 37)
    first_key, second_key, third_key = jax.random.split(key, 3)
    first_draw = jax.random.randint(first_key, (ROWS,), 1, CTX + 1)
    second_draw = jax.random.randint(second_key, (ROWS,), 1, CTX + 1)
    length_out = jnp.maximum(1, first_draw * second_draw // CTX)
    chosen = jax.random.randint(third_key, (), 0, ROWS)
    return length_out.at[chosen].set(CTX).astype(jnp.int32)


def plant(result, key, smallest, largest):
    longest = result.shape.index(max(result.shape))
    spots = []
    for shift in (0, 1):
        where = [jax.random.randint(jax.random.fold_in(key, axis), (), 0, length) for axis, length in enumerate(result.shape)]
        where[longest] = (where[longest] + shift) % result.shape[longest]
        spots.append(tuple(where))
    return result.at[spots[0]].set(smallest).at[spots[1]].set(largest)


def steps_of(own_key, extent, cuts, smallest, top_value):
    loudness, own = 1.0, jax.random.fold_in(own_key, 6)
    for axis_at, shards_of in cuts:
        steps = jnp.exp(jax.random.uniform(jax.random.fold_in(own, axis_at), (shards_of,), jnp.float32, smallest / len(cuts), top_value / len(cuts)))
        loudness = loudness * jnp.repeat(steps, extent[axis_at] // shards_of).reshape([-1 if axis == axis_at else 1 for axis in range(len(extent))])
    return loudness


def scatter_about(own_key, shape, scale, most, pieces=(), kind=jnp.bfloat16):
    array = scale * jax.random.normal(own_key, shape, jnp.float32)
    if pieces:
        array = array * steps_of(own_key, shape, pieces, -0.22, 0.18)
    return jnp.clip(array, -most, most).astype(kind)


def setup_inputs(seed: int = 0, part: int = 0) -> dict:
    seeds = jax.random.split(jax.random.key(seed), 9)
    own_keys = jax.random.split(jax.random.fold_in(seeds[8], part), 9)
    tokens = draw_tokens(jax.random.fold_in(jax.random.fold_in(seeds[8], part), 71), part)
    norm_gain = jnp.clip(1.0 + 0.18 * jax.random.normal(seeds[1], (D,), jnp.float32), 0.099609375, 1.8984375).astype(jnp.bfloat16)
    w_qkv = scatter_about(seeds[2], (D, HQ * DH + 2 * DH), D ** -0.5, 0.046875, ((1, 16),))
    key_cache = draw_key_cache(jax.random.fold_in(jax.random.fold_in(seeds[8], part), 71), part)
    value_cache = scatter_about(own_keys[4], (ROWS, CTX, DH), 1.0, 6.0, ((0, 16),))
    lengths = draw_lengths(jax.random.fold_in(jax.random.fold_in(seeds[8], part), 71), part)
    positions = plant(jax.random.randint(own_keys[6], (ROWS,), 0, CTX), jax.random.fold_in(own_keys[6], 1), 0, CTX - 1).astype(jnp.int32)
    w_out = scatter_about(seeds[7], (HQ * DH, D), (HQ * DH) ** -0.5, 0.0625, ((1, 16),))
    return dict(tokens=tokens, norm_gain=norm_gain, w_qkv=w_qkv, key_cache=key_cache, value_cache=value_cache, lengths=lengths, positions=positions, w_out=w_out)


epsilon = 1e-06

def rotary(vectors, position):
    half_size = vectors.shape[-1] // 2
    exponent = jnp.arange(half_size, dtype=jnp.float32) * (-2.0 / vectors.shape[-1])
    inverse_freq = jnp.power(jnp.float32(10000.0), exponent)
    angles = position.astype(jnp.float32)[:, None, None] * inverse_freq[None, None, :]
    cosine = jnp.cos(angles)
    sine_part = jnp.sin(angles)
    leading = vectors[..., :half_size]
    trailing = vectors[..., half_size:]
    return jnp.concatenate([leading * cosine - trailing * sine_part, trailing * cosine + leading * sine_part], axis=-1)

def reference(tokens, norm_gain, w_qkv, key_cache, value_cache, lengths, positions, w_out):
    values_in = tokens.astype(jnp.float32)
    row_mean = lax.optimization_barrier(jnp.sum(values_in, axis=1)) / D
    row_var = lax.optimization_barrier(jnp.sum(values_in * values_in, axis=1)) / D - row_mean * row_mean
    normed = ((values_in - row_mean[:, None]) * lax.rsqrt(row_var + epsilon)[:, None] * norm_gain.astype(jnp.float32)[None, :]).astype(jnp.bfloat16)
    joined = jnp.dot(normed, w_qkv, preferred_element_type=jnp.float32).astype(jnp.bfloat16)
    row_count = joined.shape[0]
    queries = rotary(joined[:, :HQ * DH].astype(jnp.float32).reshape(row_count, HQ, DH), positions).astype(jnp.bfloat16)
    new_key = rotary(joined[:, HQ * DH:HQ * DH + DH].astype(jnp.float32).reshape(row_count, 1, DH), positions).astype(jnp.bfloat16).reshape(row_count, DH)
    new_value = joined[:, HQ * DH + DH:]
    scaling = 1.0 / math.sqrt(DH)
    own_score = jnp.einsum('rhd,rd->rh', queries.astype(jnp.float32), new_key.astype(jnp.float32)) * scaling
    scores = jnp.einsum('rhd,rtd->rht', queries.astype(jnp.float32), key_cache.astype(jnp.float32)) * scaling
    slot_ids = jnp.arange(CTX, dtype=jnp.int32)
    live_mask = slot_ids[None, None, :] < lengths[:, None, None]
    scores = jnp.where(live_mask, scores, -jnp.inf)
    highest = jnp.maximum(lax.optimization_barrier(jnp.max(scores, axis=2)), own_score)
    weights = jnp.exp(scores - highest[:, :, None])
    own_weight = jnp.exp(own_score - highest)
    totals = lax.optimization_barrier(jnp.sum(weights, axis=2)) + own_weight
    probs = (weights / totals[:, :, None]).astype(jnp.bfloat16)
    own_prob = (own_weight / totals).astype(jnp.bfloat16)
    attended = jnp.einsum('rht,rtd->rhd', probs.astype(jnp.float32), value_cache.astype(jnp.float32))
    attended = attended + own_prob.astype(jnp.float32)[:, :, None] * new_value.astype(jnp.float32)[:, None, :]
    attended = attended.astype(jnp.bfloat16).reshape(row_count, HQ * DH)
    return jnp.dot(attended, w_out, preferred_element_type=jnp.float32).astype(jnp.bfloat16)
```

```python
import functools
import math

import jax
import jax.numpy as jnp
from jax import lax
from jax.experimental import pallas as pl
from jax.experimental.pallas import tpu as pltpu
from jax.sharding import PartitionSpec as P

D = 18432
HQ = 30
DH = 256
HALF = DH // 2
SLOTS = HQ + 2
OUT_CHUNKS = 6

epsilon = 1e-06

MESH = pl.DeviceIdType.MESH


def remote(src, dst, send_sem, recv_sem, peer):
    return pltpu.make_async_remote_copy(
        src_ref=src,
        dst_ref=dst,
        send_sem=send_sem,
        recv_sem=recv_sem,
        device_id={"mx": peer},
        device_id_type=MESH,
    )


class Gather:
    def __init__(self, n, me, buf, send_sems, recv_sems):
        self.n, self.me, self.buf = n, me, buf
        self.send_sems, self.recv_sems = send_sems, recv_sems
        self.outer = n // 4
        self.core = lax.rem(me, 2)
        self.b = lax.rem(me // 2, 2)
        self.a = me // 4
        self.used = 0
        self.sent = []

    def slab(self, k, other_b, other_core):
        a = lax.rem(self.a + self.outer - k, self.outer)
        b = 1 - self.b if other_b else self.b
        core = 1 - self.core if other_core else self.core
        return a * 4 + b * 2 + core

    def send(self, slab, peer):
        copy = remote(
            self.buf.at[slab],
            self.buf.at[slab],
            self.send_sems.at[self.used],
            self.recv_sems.at[slab],
            peer,
        )
        self.used += 1
        copy.start()
        self.sent.append(copy)

    def arrive(self, slab):
        remote(
            self.buf.at[slab],
            self.buf.at[slab],
            self.send_sems.at[0],
            self.recv_sems.at[slab],
            self.me,
        ).wait_recv()

    def to_a(self):
        for k in range(1, self.outer):
            a = lax.rem(self.a + k, self.outer)
            self.send(self.me, a * 4 + self.b * 2 + self.core)

    def to_b(self, slab):
        self.send(slab, self.a * 4 + (1 - self.b) * 2 + self.core)

    def to_core(self, slab):
        self.send(slab, self.a * 4 + self.b * 2 + 1 - self.core)

    def run(self, use):
        self.to_b(self.me)
        self.to_core(self.me)
        self.to_a()
        for k in range(self.outer):
            mine = self.slab(k, False, False)
            if k:
                self.arrive(mine)
                self.to_b(mine)
                self.to_core(mine)
            use(mine)
            across = self.slab(k, True, False)
            self.arrive(across)
            self.to_core(across)
            use(across)
            for other_b in (False, True):
                slab = self.slab(k, other_b, True)
                self.arrive(slab)
                use(slab)

    def finish(self):
        for copy in self.sent:
            copy.wait_send()


def n_gather_sends(n):
    return (n // 4 - 1) + n // 4 + n // 2


def kernel(
    n, x_ref, gain_ref, w_hbm, k_hbm, v_hbm, len_ref, cos_ref, sin_ref, wo_hbm, out_ref,
    stats, xg, w_v, acc, joined_out, joined_in, joined_2d, k_v, v_v, heads_first, att,
    att_2d, wo_v, total,
    w_sems, kv_sems, wo_sems, st_send, st_recv, x_send, x_recv, j_send, j_recv, a_send, a_recv,
):
    me = lax.axis_index("mx")
    rows, features = x_ref.shape
    columns = w_hbm.shape[1]
    local = k_hbm.shape[0]
    context = k_hbm.shape[1]

    barrier = pltpu.get_barrier_semaphore()

    def greet(k, carry):
        pl.semaphore_signal(
            barrier, inc=1, device_id={"mx": lax.rem(me + k, n)}, device_id_type=MESH
        )
        return carry

    lax.fori_loop(1, n, greet, 0)

    gather = Gather(n, me, xg, x_send, x_recv)

    def w_copy(slab):
        start = pl.multiple_of(slab * features, features)
        return pltpu.make_async_copy(
            w_hbm.at[pl.ds(start, features), :], w_v.at[slab], w_sems.at[slab]
        )

    for k in range(gather.outer):
        for other_core in (False, True):
            for other_b in (False, True):
                w_copy(gather.slab(k, other_b, other_core)).start()
    k_copy = pltpu.make_async_copy(k_hbm, k_v, kv_sems.at[0])
    v_copy = pltpu.make_async_copy(v_hbm, v_v, kv_sems.at[1])
    k_copy.start()
    v_copy.start()
    depth = wo_hbm.shape[0] // OUT_CHUNKS
    wo_copies = [
        pltpu.make_async_copy(
            wo_hbm.at[pl.ds(i * depth, depth), :], wo_v.at[i], wo_sems.at[i]
        )
        for i in range(OUT_CHUNKS)
    ]
    for copy in wo_copies:
        copy.start()

    x = x_ref[...].astype(jnp.float32)
    eye = lax.broadcasted_iota(jnp.int32, (rows, rows), 0) == lax.broadcasted_iota(
        jnp.int32, (rows, rows), 1
    )

    def as_row(column):
        return jnp.sum(jnp.where(eye, column, 0.0), axis=0, keepdims=True)

    def as_column(row):
        return jnp.sum(jnp.where(eye, row, 0.0), axis=1, keepdims=True)

    stats[me, 0:1, :] = as_row(jnp.sum(x, axis=1, keepdims=True))
    stats[me, 1:2, :] = as_row(jnp.sum(x * x, axis=1, keepdims=True))

    pl.semaphore_wait(barrier, n - 1)

    def st_copy(k):
        return remote(
            stats.at[me], stats.at[me], st_send.at[k], st_recv.at[me], lax.rem(me + k, n)
        )

    def start_stats(k, carry):
        st_copy(k).start()
        return carry

    def wait_stats(k, carry):
        source = lax.rem(me + k, n)
        remote(
            stats.at[source], stats.at[source], st_send.at[k], st_recv.at[source], me
        ).wait_recv()
        return carry

    lax.fori_loop(1, n, start_stats, 0)
    acc[...] = jnp.zeros_like(acc)
    lax.fori_loop(1, n, wait_stats, 0)
    sums = jnp.sum(stats[...], axis=0)
    row_mean = sums[0:1, :] / D
    row_var = sums[1:2, :] / D - row_mean * row_mean
    scale = as_column(lax.rsqrt(row_var + epsilon))
    shift = as_column(row_mean)
    xg[me] = ((x - shift) * scale * gain_ref[...].astype(jnp.float32)).astype(jnp.bfloat16)

    def project(slab):
        w_copy(slab).wait()
        acc[...] += jnp.dot(xg[slab], w_v[slab], preferred_element_type=jnp.float32)

    gather.run(project)

    for j in range(n):
        joined_out[j] = acc[j * local : (j + 1) * local, :].astype(jnp.bfloat16)
    joined_in[me] = joined_out[me]

    def j_copy(k):
        peer = lax.rem(me + k, n)
        return remote(
            joined_out.at[peer], joined_in.at[me], j_send.at[k], j_recv.at[me], peer
        )

    def start_joined(k, carry):
        j_copy(k).start()
        return carry

    def wait_joined(k, carry):
        source = lax.rem(me + k, n)
        remote(
            joined_out.at[source], joined_in.at[source], j_send.at[k], j_recv.at[source], me
        ).wait_recv()
        return carry

    lax.fori_loop(1, n, start_joined, 0)
    lax.fori_loop(1, n, wait_joined, 0)
    for j in range(n):
        joined_2d[j * local : (j + 1) * local, :] = joined_in[j].astype(jnp.float32)

    pieces = columns // HALF
    shape = (local * SLOTS, n * local)
    to_row = lax.broadcasted_iota(jnp.int32, shape, 0)
    from_row = lax.broadcasted_iota(jnp.int32, shape, 1)
    same_row = to_row // SLOTS == from_row % local
    to_piece = 2 * (to_row % SLOTS)
    from_piece = pieces * (from_row // local)
    halves = []
    for part in range(2):
        half = jnp.zeros((local * SLOTS, HALF), jnp.float32)
        for piece in range(pieces):
            if pieces % 2 == 0 and piece % 2 != part:
                continue
            chosen = same_row & (from_piece + piece == to_piece + part)
            half += jnp.dot(
                jnp.where(chosen, 1.0, 0.0).astype(jnp.bfloat16),
                joined_2d[:, piece * HALF : (piece + 1) * HALF].astype(jnp.bfloat16),
                preferred_element_type=jnp.float32,
            )
        halves.append(half)

    k_copy.wait()
    v_copy.wait()
    scaling = 1.0 / math.sqrt(DH)
    slot_ids = lax.broadcasted_iota(jnp.int32, (SLOTS, context), 1)
    results = []
    for r in range(local):
        leading = halves[0][r * SLOTS : (r + 1) * SLOTS]
        trailing = halves[1][r * SLOTS : (r + 1) * SLOTS]
        cosine = cos_ref[r : r + 1, :]
        sine = sin_ref[r : r + 1, :]
        rotated = jnp.concatenate(
            [leading * cosine - trailing * sine, trailing * cosine + leading * sine], axis=1
        ).astype(jnp.bfloat16)
        new_value = jnp.concatenate(
            [leading[SLOTS - 1 : SLOTS], trailing[SLOTS - 1 : SLOTS]], axis=1
        )
        wide = rotated.astype(jnp.float32)
        own = jnp.sum(wide * wide[HQ : HQ + 1], axis=1, keepdims=True) * scaling
        scores = (
            lax.dot_general(
                rotated, k_v[r], (((1,), (1,)), ((), ())), preferred_element_type=jnp.float32
            )
            * scaling
        )
        scores = jnp.where(slot_ids < len_ref[r], scores, -jnp.inf)
        highest = jnp.maximum(jnp.max(scores, axis=1, keepdims=True), own)
        weights = jnp.exp(scores - highest)
        own_weight = jnp.exp(own - highest)
        totals = jnp.sum(weights, axis=1, keepdims=True) + own_weight
        inverse = 1.0 / totals
        probs = (weights * inverse).astype(jnp.bfloat16)
        own_prob = (own_weight * inverse).astype(jnp.bfloat16).astype(jnp.float32)
        attended = jnp.dot(probs, v_v[r], preferred_element_type=jnp.float32)
        results.append((attended + own_prob * new_value).astype(jnp.bfloat16))
    stacked = jnp.concatenate(results, axis=0)

    square = (local * SLOTS, local * SLOTS)
    to_row = lax.broadcasted_iota(jnp.int32, square, 0)
    from_row = lax.broadcasted_iota(jnp.int32, square, 1)
    swap = (to_row // local == from_row % SLOTS) & (to_row % local == from_row // SLOTS)
    heads_first[...] = jnp.dot(
        jnp.where(swap, 1.0, 0.0).astype(jnp.bfloat16),
        stacked,
        preferred_element_type=jnp.float32,
    )
    for h in range(HQ):
        att[me, :, h * DH : (h + 1) * DH] = heads_first[
            h * local : (h + 1) * local, :
        ].astype(jnp.bfloat16)

    spread = Gather(n, me, att, a_send, a_recv)
    spread.run(lambda slab: None)

    for j in range(n):
        att_2d[j * local : (j + 1) * local, :] = att[j].astype(jnp.float32)
    for i, copy in enumerate(wo_copies):
        copy.wait()
        product = jnp.dot(
            att_2d[:, i * depth : (i + 1) * depth].astype(jnp.bfloat16),
            wo_v[i],
            preferred_element_type=jnp.float32,
        )
        if i == 0:
            total[...] = product
        elif i < OUT_CHUNKS - 1:
            total[...] += product
        else:
            out_ref[...] = (total[...] + product).astype(jnp.bfloat16)

    def finish(k, carry):
        st_copy(k).wait_send()
        j_copy(k).wait_send()
        return carry

    lax.fori_loop(1, n, finish, 0)
    gather.finish()
    spread.finish()


def shards(n, tokens, norm_gain, w_qkv, key_cache, value_cache, lengths, positions, w_out):
    rows, features = tokens.shape
    columns = w_qkv.shape[1]
    local, context, _ = key_cache.shape
    inner, width = w_out.shape
    exponent = jnp.arange(HALF, dtype=jnp.float32) * (-2.0 / DH)
    inverse_freq = jnp.power(jnp.float32(10000.0), exponent)
    angles = positions.astype(jnp.float32)[:, None] * inverse_freq[None, :]
    bf16, f32 = jnp.bfloat16, jnp.float32
    vmem = pl.BlockSpec(memory_space=pltpu.VMEM)
    smem = pl.BlockSpec(memory_space=pltpu.SMEM)
    hbm = pl.BlockSpec(memory_space=pl.ANY)
    dma = pltpu.SemaphoreType.DMA
    sends = n_gather_sends(n)
    return pl.pallas_call(
        functools.partial(kernel, n),
        out_shape=jax.ShapeDtypeStruct((rows, width), bf16),
        in_specs=[vmem, vmem, hbm, hbm, hbm, smem, vmem, vmem, hbm],
        out_specs=vmem,
        scratch_shapes=[
            pltpu.VMEM((n, 2, rows), f32),
            pltpu.VMEM((n, rows, features), bf16),
            pltpu.VMEM((n, features, columns), bf16),
            pltpu.VMEM((rows, columns), f32),
            pltpu.VMEM((n, local, columns), bf16),
            pltpu.VMEM((n, local, columns), bf16),
            pltpu.VMEM((rows, columns), f32),
            pltpu.VMEM((local, context, DH), bf16),
            pltpu.VMEM((local, context, DH), bf16),
            pltpu.VMEM((local * SLOTS, DH), f32),
            pltpu.VMEM((n, local, inner), bf16),
            pltpu.VMEM((rows, inner), f32),
            pltpu.VMEM((OUT_CHUNKS, inner // OUT_CHUNKS, width), bf16),
            pltpu.VMEM((rows, width), f32),
            dma((n,)),
            dma((2,)),
            dma((OUT_CHUNKS,)),
            dma((n,)),
            dma((n,)),
            dma((sends,)),
            dma((n,)),
            dma((n,)),
            dma((n,)),
            dma((sends,)),
            dma((n,)),
        ],
        compiler_params=pltpu.CompilerParams(
            collective_id=0, has_side_effects=True, vmem_limit_bytes=60 * 1024 * 1024
        ),
    )(
        tokens, norm_gain.reshape(1, features), w_qkv, key_cache, value_cache, lengths,
        jnp.cos(angles), jnp.sin(angles), w_out,
    )


def solution(mesh):
    placed = (
        P("groups", "mx"),
        P("mx"),
        P(None, "mx"),
        P(("groups", "mx"), None, None),
        P(("groups", "mx"), None, None),
        P(("groups", "mx")),
        P(("groups", "mx")),
        P(None, "mx"),
    )
    return jax.shard_map(
        functools.partial(shards, mesh.shape["mx"]),
        mesh=mesh,
        in_specs=placed,
        out_specs=P("groups", "mx"),
        check_vma=False,
    )
```

```python
import functools
import math

import jax
import jax.numpy as jnp
from jax import lax
from jax.experimental import pallas as pl
from jax.experimental.pallas import tpu as pltpu
from jax.sharding import PartitionSpec as P

D = 18432
HQ = 30
DH = 256
HALF = DH // 2
SLOTS = HQ + 2
OUT_CHUNKS = 4
X_CHUNKS = 2

epsilon = 1e-06

MESH = pl.DeviceIdType.MESH


def remote(src, dst, send_sem, recv_sem, peer):
    return pltpu.make_async_remote_copy(
        src_ref=src,
        dst_ref=dst,
        send_sem=send_sem,
        recv_sem=recv_sem,
        device_id={"mx": peer},
        device_id_type=MESH,
    )


class Gather:
    def __init__(self, n, me, buf, chunks, send_sems, recv_sems):
        self.n, self.me, self.buf = n, me, buf
        self.send_sems, self.recv_sems = send_sems, recv_sems
        self.outer = n // 4
        self.core = lax.rem(me, 2)
        self.b = lax.rem(me // 2, 2)
        self.a = me // 4
        self.chunks = chunks
        self.depth = buf.shape[1] // chunks

    def index(self, a, other_b, other_core):
        b = 1 - self.b if other_b else self.b
        core = 1 - self.core if other_core else self.core
        return a * 4 + b * 2 + core

    def copy(self, slab, chunk, kind, peer):
        part = self.buf.at[slab, pl.ds(chunk * self.depth, self.depth), :]
        return remote(
            part, part, self.send_sems.at[kind, slab, chunk], self.recv_sems.at[slab, chunk], peer
        )

    def out(self, a, chunk, kind, other_b=False, wait=False):
        slab = self.index(a, other_b, False)
        ahead = {0: self.a - 1, 1: self.a + 1}.get(kind, self.a)
        peer = self.index(ahead, kind == 2, kind == 3)

        def go():
            copy = self.copy(slab, chunk, kind, peer)
            if wait:
                copy.wait_send()
            else:
                copy.start()

        if kind == 0:
            pl.when((self.a > 0) & (a >= self.a))(go)
        elif kind == 1:
            pl.when((self.a < self.outer - 1) & (a <= self.a))(go)
        else:
            go()

    def arrive(self, slab, chunk):
        self.copy(slab, chunk, 0, self.me).wait_recv()

    def order(self):
        for step in range(1, self.outer):
            yield self.a - step, self.a - step >= 0
            yield self.a + step, self.a + step < self.outer

    def each(self, act):
        act(self.a)
        for a, there in self.order():
            pl.when(there)(functools.partial(act, a))

    def run(self, use):
        def forward(a, chunk):
            for kind in (0, 1, 2, 3):
                self.out(a, chunk, kind)

        for chunk in range(self.chunks):
            forward(self.a, chunk)

        def mine(a):
            for chunk in range(self.chunks):
                self.arrive(self.index(a, False, False), chunk)
                forward(a, chunk)

        def across(a):
            for chunk in range(self.chunks):
                self.arrive(self.index(a, True, False), chunk)
                self.out(a, chunk, 3, other_b=True)

        def beside(a):
            for other_b in (False, True):
                slab = self.index(a, other_b, True)
                for chunk in range(self.chunks):
                    self.arrive(slab, chunk)
                use(slab)

        def settle(a):
            across(a)
            use(self.index(a, False, False))
            use(self.index(a, True, False))
            beside(a)

        places = list(self.order())
        for step in range(self.outer):
            for a, there in places[2 * step : 2 * step + 2]:
                pl.when(there)(functools.partial(mine, a))
            if step == 0:
                settle(self.a)
            for a, there in places[2 * step - 2 : 2 * step] if step else []:
                pl.when(there)(functools.partial(settle, a))

    def finish(self):
        def act(a):
            for chunk in range(self.chunks):
                for kind in (0, 1, 2, 3):
                    self.out(a, chunk, kind, wait=True)
                self.out(a, chunk, 3, other_b=True, wait=True)

        self.each(act)


def kernel(
    n, x_ref, gain_ref, w_hbm, k_hbm, v_hbm, len_ref, cos_ref, sin_ref, wo_hbm, out_ref,
    stats, xg, w_v, acc, joined_f32, joined_out, joined_in, joined_2d, k_v, v_v, heads_first,
    att_f32, att, wo_v, total,
    w_sems, kv_sems, wo_sems, st_send, st_recv, x_send, x_recv, j_send, j_recv, a_send, a_recv,
):
    me = lax.axis_index("mx")
    rows, features = x_ref.shape
    columns = w_hbm.shape[1]
    local = k_hbm.shape[0]
    context = k_hbm.shape[1]

    barrier = pltpu.get_barrier_semaphore()

    def greet(k, carry):
        pl.semaphore_signal(
            barrier, inc=1, device_id={"mx": lax.rem(me + k, n)}, device_id_type=MESH
        )
        return carry

    lax.fori_loop(1, n, greet, 0)

    gather = Gather(n, me, xg, X_CHUNKS, x_send, x_recv)

    def w_copy(slab):
        start = pl.multiple_of(slab * features, features)
        return pltpu.make_async_copy(
            w_hbm.at[pl.ds(start, features), :], w_v.at[slab], w_sems.at[slab]
        )

    def fetch(a):
        for other_core in (False, True):
            for other_b in (False, True):
                w_copy(gather.index(a, other_b, other_core)).start()

    gather.each(fetch)
    k_copy = pltpu.make_async_copy(k_hbm, k_v, kv_sems.at[0])
    v_copy = pltpu.make_async_copy(v_hbm, v_v, kv_sems.at[1])
    k_copy.start()
    v_copy.start()
    depth = wo_hbm.shape[0] // OUT_CHUNKS
    wo_copies = [
        pltpu.make_async_copy(
            wo_hbm.at[pl.ds(i * depth, depth), :], wo_v.at[i], wo_sems.at[i]
        )
        for i in range(OUT_CHUNKS)
    ]
    for copy in wo_copies:
        copy.start()

    x = x_ref[...].astype(jnp.float32)
    eye = lax.broadcasted_iota(jnp.int32, (rows, rows), 0) == lax.broadcasted_iota(
        jnp.int32, (rows, rows), 1
    )

    def as_row(column):
        return jnp.sum(jnp.where(eye, column, 0.0), axis=0, keepdims=True)

    def as_column(row):
        return jnp.sum(jnp.where(eye, row, 0.0), axis=1, keepdims=True)

    stats[me, 0:1, :] = as_row(jnp.sum(x, axis=1, keepdims=True))
    stats[me, 1:2, :] = as_row(jnp.sum(x * x, axis=1, keepdims=True))

    pl.semaphore_wait(barrier, n - 1)

    def st_copy(k):
        return remote(
            stats.at[me], stats.at[me], st_send.at[k], st_recv.at[me], lax.rem(me + k, n)
        )

    def start_stats(k, carry):
        st_copy(k).start()
        return carry

    def wait_stats(k, carry):
        source = lax.rem(me + k, n)
        remote(
            stats.at[source], stats.at[source], st_send.at[k], st_recv.at[source], me
        ).wait_recv()
        return carry

    lax.fori_loop(1, n, start_stats, 0)
    acc[...] = jnp.zeros_like(acc)
    lax.fori_loop(1, n, wait_stats, 0)
    sums = jnp.sum(stats[...], axis=0)
    row_mean = sums[0:1, :] / D
    row_var = sums[1:2, :] / D - row_mean * row_mean
    scale = as_column(lax.rsqrt(row_var + epsilon))
    shift = as_column(row_mean)
    xg[me] = ((x - shift) * scale * gain_ref[...].astype(jnp.float32)).astype(jnp.bfloat16)

    def project(slab):
        w_copy(slab).wait()
        acc[...] += jnp.dot(xg[slab], w_v[slab], preferred_element_type=jnp.float32)

    gather.run(project)

    pieces = columns // HALF
    for j in range(n):
        for piece in range(pieces):
            joined_f32[j, piece * local : (piece + 1) * local, :] = acc[
                j * local : (j + 1) * local, piece * HALF : (piece + 1) * HALF
            ]
    joined_out[...] = joined_f32[...].astype(jnp.bfloat16)
    joined_in[me] = joined_out[me]

    def j_copy(k):
        peer = lax.rem(me + k, n)
        return remote(
            joined_out.at[peer], joined_in.at[me], j_send.at[k], j_recv.at[me], peer
        )

    def start_joined(k, carry):
        j_copy(k).start()
        return carry

    def wait_joined(k, carry):
        source = lax.rem(me + k, n)
        remote(
            joined_out.at[source], joined_in.at[source], j_send.at[k], j_recv.at[source], me
        ).wait_recv()
        return carry

    lax.fori_loop(1, n, start_joined, 0)
    lax.fori_loop(1, n, wait_joined, 0)
    width = pieces * local
    if width % 16 == 0:
        moved = joined_in[...].reshape(n * width, HALF)
    else:
        for j in range(n):
            joined_2d[j * width : (j + 1) * width, :] = joined_in[j].astype(jnp.float32)
        moved = joined_2d[...].astype(jnp.bfloat16)

    shape = (local * SLOTS, n * width)
    to_row = lax.broadcasted_iota(jnp.int32, shape, 0)
    source = lax.broadcasted_iota(jnp.int32, shape, 1)
    same_row = to_row // SLOTS == source % local
    halves = []
    for part in range(2):
        chosen = same_row & (source // local == 2 * (to_row % SLOTS) + part)
        halves.append(
            jnp.dot(
                jnp.where(chosen, 1.0, 0.0).astype(jnp.bfloat16),
                moved,
                preferred_element_type=jnp.float32,
            )
        )

    k_copy.wait()
    v_copy.wait()
    scaling = 1.0 / math.sqrt(DH)
    slot_ids = lax.broadcasted_iota(jnp.int32, (SLOTS, context), 1)
    results = []
    for r in range(local):
        leading = halves[0][r * SLOTS : (r + 1) * SLOTS]
        trailing = halves[1][r * SLOTS : (r + 1) * SLOTS]
        cosine = cos_ref[r : r + 1, :]
        sine = sin_ref[r : r + 1, :]
        rotated = jnp.concatenate(
            [leading * cosine - trailing * sine, trailing * cosine + leading * sine], axis=1
        ).astype(jnp.bfloat16)
        new_value = jnp.concatenate(
            [leading[SLOTS - 1 : SLOTS], trailing[SLOTS - 1 : SLOTS]], axis=1
        )
        wide = rotated.astype(jnp.float32)
        own = jnp.sum(wide * wide[HQ : HQ + 1], axis=1, keepdims=True) * scaling
        scores = (
            lax.dot_general(
                rotated, k_v[r], (((1,), (1,)), ((), ())), preferred_element_type=jnp.float32
            )
            * scaling
        )
        scores = jnp.where(slot_ids < len_ref[r], scores, -jnp.inf)
        highest = jnp.maximum(jnp.max(scores, axis=1, keepdims=True), own)
        weights = jnp.exp(scores - highest)
        own_weight = jnp.exp(own - highest)
        totals = jnp.sum(weights, axis=1, keepdims=True) + own_weight
        inverse = 1.0 / totals
        probs = (weights * inverse).astype(jnp.bfloat16)
        own_prob = (own_weight * inverse).astype(jnp.bfloat16).astype(jnp.float32)
        attended = jnp.dot(probs, v_v[r], preferred_element_type=jnp.float32)
        results.append((attended + own_prob * new_value).astype(jnp.bfloat16))
    stacked = jnp.concatenate(results, axis=0)

    square = (local * SLOTS, local * SLOTS)
    to_row = lax.broadcasted_iota(jnp.int32, square, 0)
    from_row = lax.broadcasted_iota(jnp.int32, square, 1)
    swap = (to_row // local == from_row % SLOTS) & (to_row % local == from_row // SLOTS)
    heads_first[...] = jnp.dot(
        jnp.where(swap, 1.0, 0.0).astype(jnp.bfloat16),
        stacked,
        preferred_element_type=jnp.float32,
    )
    quarter = att.shape[2]
    per_quarter = quarter // HALF
    for h in range(HQ):
        for part in range(2):
            at, place = (2 * h + part) // per_quarter, (2 * h + part) % per_quarter
            att_f32[at * local : (at + 1) * local, place * HALF : (place + 1) * HALF] = heads_first[
                h * local : (h + 1) * local, part * HALF : (part + 1) * HALF
            ]
    att[me] = att_f32[...].astype(jnp.bfloat16)

    spread = Gather(n, me, att, 1, a_send, a_recv)
    spread.run(lambda slab: None)

    height = att.shape[1]
    gathered = att[...].reshape(n * height, quarter)
    shape = (rows, n * height)
    to_row = lax.broadcasted_iota(jnp.int32, shape, 0)
    source = lax.broadcasted_iota(jnp.int32, shape, 1)
    same_row = (to_row // local == source // height) & (to_row % local == source % local)
    for i, copy in enumerate(wo_copies):
        chosen = same_row & (source % height // local == i)
        part = jnp.dot(
            jnp.where(chosen, 1.0, 0.0).astype(jnp.bfloat16),
            gathered,
            preferred_element_type=jnp.float32,
        ).astype(jnp.bfloat16)
        copy.wait()
        product = jnp.dot(part, wo_v[i], preferred_element_type=jnp.float32)
        if i == 0:
            total[...] = product
        elif i < OUT_CHUNKS - 1:
            total[...] += product
        else:
            out_ref[...] = (total[...] + product).astype(jnp.bfloat16)

    def finish(k, carry):
        st_copy(k).wait_send()
        j_copy(k).wait_send()
        return carry

    lax.fori_loop(1, n, finish, 0)
    gather.finish()
    spread.finish()


def shards(n, tokens, norm_gain, w_qkv, key_cache, value_cache, lengths, positions, w_out):
    rows, features = tokens.shape
    columns = w_qkv.shape[1]
    local, context, _ = key_cache.shape
    inner, width = w_out.shape
    exponent = jnp.arange(HALF, dtype=jnp.float32) * (-2.0 / DH)
    inverse_freq = jnp.power(jnp.float32(10000.0), exponent)
    angles = positions.astype(jnp.float32)[:, None] * inverse_freq[None, :]
    bf16, f32 = jnp.bfloat16, jnp.float32
    vmem = pl.BlockSpec(memory_space=pltpu.VMEM)
    smem = pl.BlockSpec(memory_space=pltpu.SMEM)
    hbm = pl.BlockSpec(memory_space=pl.ANY)
    dma = pltpu.SemaphoreType.DMA
    pieces = columns // HALF
    return pl.pallas_call(
        functools.partial(kernel, n),
        out_shape=jax.ShapeDtypeStruct((rows, width), bf16),
        in_specs=[vmem, vmem, hbm, hbm, hbm, smem, vmem, vmem, hbm],
        out_specs=vmem,
        scratch_shapes=[
            pltpu.VMEM((n, 2, rows), f32),
            pltpu.VMEM((n, rows, features), bf16),
            pltpu.VMEM((n, features, columns), bf16),
            pltpu.VMEM((rows, columns), f32),
            pltpu.VMEM((n, pieces * local, HALF), f32),
            pltpu.VMEM((n, pieces * local, HALF), bf16),
            pltpu.VMEM((n, pieces * local, HALF), bf16),
            pltpu.VMEM((n * pieces * local, HALF), f32),
            pltpu.VMEM((local, context, DH), bf16),
            pltpu.VMEM((local, context, DH), bf16),
            pltpu.VMEM((local * SLOTS, DH), f32),
            pltpu.VMEM((OUT_CHUNKS * local, inner // OUT_CHUNKS), f32),
            pltpu.VMEM((n, OUT_CHUNKS * local, inner // OUT_CHUNKS), bf16),
            pltpu.VMEM((OUT_CHUNKS, inner // OUT_CHUNKS, width), bf16),
            pltpu.VMEM((rows, width), f32),
            dma((n,)),
            dma((2,)),
            dma((OUT_CHUNKS,)),
            dma((n,)),
            dma((n,)),
            dma((4, n, X_CHUNKS)),
            dma((n, X_CHUNKS)),
            dma((n,)),
            dma((n,)),
            dma((4, n, 1)),
            dma((n, 1)),
        ],
        compiler_params=pltpu.CompilerParams(
            collective_id=0, has_side_effects=True, vmem_limit_bytes=60 * 1024 * 1024
        ),
    )(
        tokens, norm_gain.reshape(1, features), w_qkv, key_cache, value_cache, lengths,
        jnp.cos(angles), jnp.sin(angles), w_out,
    )


def solution(mesh):
    placed = (
        P("groups", "mx"),
        P("mx"),
        P(None, "mx"),
        P(("groups", "mx"), None, None),
        P(("groups", "mx"), None, None),
        P(("groups", "mx")),
        P(("groups", "mx")),
        P(None, "mx"),
    )
    return jax.shard_map(
        functools.partial(shards, mesh.shape["mx"]),
        mesh=mesh,
        in_specs=placed,
        out_specs=P("groups", "mx"),
        check_vma=False,
    )
```
